512 devices in a mesh: dp: 16 (over z_lo, x), expert: 32 (over y, z_hi, core).
Axes of the slice: x: 4, y: 4, z: 16 (z_hi: 4, z_lo: 4; z = z_hi * 4 + z_lo), core: 2. Of those that a mesh axis runs over, the one named last changes fastest.
Arguments:
- tokens: bfloat16 [65536, 2560], P(('dp', 'expert')), may hold values from -6 to 6
- cotangent: bfloat16 [65536, 2560], P(('dp', 'expert')), may hold values from -6 to 6
- expert_ids: int32 [65536, 2], P(('dp', 'expert')), may hold values from 0 to 31, all different within a row; in each aligned block of 128 rows (0 to 127, 128 to 255, ...) at most 9 rows name the same one
- gate_values: float32 [65536, 2], P(('dp', 'expert')), may hold values from 0.05 to 1
- w_gate: bfloat16 [32, 768, 2560], P('expert', 'dp'), may hold values from -0.125 to 0.125
- w_up: bfloat16 [32, 768, 2560], P('expert', 'dp'), may hold values from -0.125 to 0.125
- w_down: bfloat16 [32, 768, 2560], P('expert', 'dp'), may hold values from -0.21875 to 0.21875
Outputs:
- token_grad: bfloat16 [65536, 2560], P(('dp', 'expert'))
- gate_grad: float32 [65536, 2], P(('dp', 'expert'))
The draws below stay inside these ranges and needn't reach their ends.
Inputs may be any that keep to these rules, and one draw needn't show every extreme that they name: `expert_ids`: each row names 2 different experts. Among the rows of one device (128 aligned rows), no expert is named by more than 9 rows, and in some blocks one expert is named by exactly 9.
All inputs are finite; a program needn't handle non-finite values.
Results may differ from the reference program's by a relative error of at most 0.02.
Values may be sent and summed in bfloat16 or wider, within the bound.
No kernel may reach another device: no remote copies, remote signals or barrier semaphores. Data moves between devices by JAX's collectives and lax.ppermute only.
A program may use at most 128 MiB of HBM per device.

```python
import math
import jax
import jax.numpy as jnp
import numpy as np
from jax import lax

D = 2560
FF = 768
TOP_K = 2
TOK_DEV = 128
EXPERTS = 32
CAP = 9
TOKENS = 65536


def block_levels(key, shape, cuts, least, high):
    level, own = 1.0, jax.random.fold_in(key, 6)
    for axis_at, blocks in cuts:
        steps = jnp.exp(jax.random.uniform(jax.random.fold_in(own, axis_at), (blocks,), jnp.float32, least / len(cuts), high / len(cuts)))
        level = level * jnp.repeat(steps, shape[axis_at] // blocks).reshape([-1 if axis == axis_at else 1 for axis in range(len(shape))])
    return level


def shared_out(stream_key, own, number, rows, number_of, top, limit, skew):
    ranking = jax.random.permutation(stream_key, number_of)
    heavy_load, usual = shares(number_of, rows * top, limit, skew, True), shares(number_of, rows * top, limit, skew, False)
    places = jnp.arange(number_of)

    def named(sizes, turn):
        used = int((sizes > 0).sum())
        fixed = max(1, used // 4)
        shifted = fixed + (places - fixed + turn * (used - fixed)) % max(1, number_of - fixed)
        return jnp.zeros((number_of,), jnp.int32).at[ranking[jnp.where(places < fixed, places, shifted)]].set(jnp.asarray(sizes, jnp.int32))

    sizes = jnp.where(number % 4 == 0, named(heavy_load, number // 4), named(usual, number - number // 4 - 1))
    mixed = jax.random.permutation(jax.random.fold_in(own, 3), number_of)
    donor, sink = mixed[0:number_of // 2 * 2:2], mixed[1:number_of // 2 * 2:2]
    margin = jnp.minimum(sizes[donor] - 1, limit - sizes[sink]) // 2
    margin = jnp.where((donor == ranking[0]) | (sink == ranking[0]) | (sizes[sink] == 0), 0, jnp.maximum(margin, 0))
    shifted = jax.random.randint(jax.random.fold_in(own, 4), (number_of // 2,), 0, 1 << 20) % (margin + 1)
    sizes = sizes.at[donor].add(-shifted).at[sink].add(shifted)
    labels = jnp.searchsorted(jnp.cumsum(sizes), jnp.arange(rows * top), side="right").astype(jnp.int32)
    grid = labels.reshape(top, rows).T
    grid = grid[jax.random.permutation(jax.random.fold_in(own, 1), rows)]
    turn = jax.random.randint(jax.random.fold_in(own, 2), (rows, 1), 0, top)
    return jnp.take_along_axis(grid, (jnp.arange(top)[None, :] + turn) % top, axis=1)


def shares(amount, total, limit, skew, full):
    weights = [(1 << 20) // math.isqrt(rank ** skew) + 1 for rank in range(1, amount + 1)]
    largest = limit if full else min(limit, max(-(-total // amount), total * weights[0] // sum(weights)))
    least = 1 if total - largest >= amount - 1 else 0
    given, spare = [largest] + [least] * (amount - 1), total - largest - least * (amount - 1)
    while spare > 0:
        movable = [i for i in range(1, amount) if given[i] < largest] or [i for i in range(1, amount) if given[i] < limit]
        mass, remaining = sum([weights[i] for i in movable]), spare
        for i in movable:
            addition = min(limit - given[i], max(1, remaining * weights[i] // mass), spare)
            given[i] = given[i] + addition
            spare = spare - addition
    return np.array(given)


def gaussian(own_key, extent, deviation, bound, pieces=(), held_as=jnp.bfloat16):
    result = jax.random.normal(own_key, extent, jnp.float32) * deviation
    if len(pieces) > 0:
        result = block_levels(own_key, extent, pieces, -0.22, 0.18) * result
    return jnp.clip(result, min=-bound, max=bound).astype(held_as)


def setup_inputs(seed: int = 0) -> dict:
    key_list = jax.random.split(jax.random.key(seed), 8)
    tokens = gaussian(key_list[0], (TOKENS, D), 1.0, 6.0, ((0, 512),))
    cotangent = gaussian(key_list[1], (TOKENS, D), 1.0, 6.0, ((0, 512),))
    expert_ids_keys = jax.random.split(jax.random.fold_in(key_list[2], 1), TOKENS // TOK_DEV)
    expert_ids_turns = jax.random.permutation(jax.random.fold_in(key_list[2], 3), TOKENS // TOK_DEV)
    expert_ids = jax.vmap(lambda own, number: shared_out(jax.random.fold_in(key_list[2], 2), own, number, TOK_DEV, EXPERTS, TOP_K, CAP, 2))(expert_ids_keys, expert_ids_turns).reshape((TOKENS, TOP_K))
    gate_values = jnp.clip(0.05 + 0.95 * jax.random.uniform(key_list[3], (TOKENS, TOP_K), jnp.float32) ** block_levels(key_list[3], (TOKENS, TOP_K), ((0, 512),), -0.2, 0.2), 0.05, 1.0)
    w_gate = gaussian(key_list[4], (EXPERTS, FF, D), D ** -0.5, 0.125, ((0, 32), (1, 16)))
    w_up = gaussian(key_list[5], (EXPERTS, FF, D), D ** -0.5, 0.125, ((0, 32), (1, 16)))
    w_down = gaussian(key_list[6], (EXPERTS, FF, D), FF ** -0.5, 0.21875, ((0, 32), (1, 16)))
    return {"tokens": tokens, "cotangent": cotangent, "expert_ids": expert_ids, "gate_values": gate_values, "w_gate": w_gate, "w_up": w_up, "w_down": w_down}


def reference(tokens, cotangent, expert_ids, gate_values, w_gate, w_up, w_down):
    blocks = TOKENS // TOK_DEV
    width_k = TOK_DEV * TOP_K
    flat = expert_ids.reshape(blocks, width_k)
    onehot = (flat[..., None] == jnp.arange(EXPERTS, dtype=jnp.int32)[None, None, :]).astype(jnp.int32)
    before = jnp.cumsum(onehot, axis=1) - onehot
    slot = jnp.sum(before * onehot, axis=-1).astype(jnp.int32)
    place = (jnp.arange(blocks, dtype=jnp.int32)[:, None] * CAP + slot).astype(jnp.int32)
    assign = jnp.arange(TOKENS * TOP_K, dtype=jnp.int32).reshape(blocks, width_k)
    table = jnp.full((EXPERTS, blocks * CAP), -1, jnp.int32)
    table = table.at[flat.reshape(-1), place.reshape(-1)].set(assign.reshape(-1))
    gate_flat = gate_values.reshape(-1)

    def step(carry, inputs):
        grad_acc, gate_acc = carry
        column, wg, wu, wd = inputs
        valid = column >= 0
        safe = jnp.where(valid, column, 0).astype(jnp.int32)
        owner = (safe // TOP_K).astype(jnp.int32)
        rows_x = jnp.where(valid[:, None], tokens[owner], jnp.zeros((), jnp.bfloat16))
        rows_dy = jnp.where(valid[:, None], cotangent[owner], jnp.zeros((), jnp.bfloat16))
        rows_g = jnp.where(valid, gate_flat[safe], jnp.float32(0.0))
        pre_gate = jnp.dot(rows_x, wg.T, preferred_element_type=jnp.float32)
        pre_up = jnp.dot(rows_x, wu.T, preferred_element_type=jnp.float32)
        sigma = jax.nn.sigmoid(pre_gate)
        hidden = (pre_gate * sigma * pre_up).astype(jnp.bfloat16)
        expert_out = jnp.dot(hidden, wd, preferred_element_type=jnp.float32)
        gate_term = jnp.sum(expert_out * rows_dy.astype(jnp.float32), axis=-1)
        scaled = (rows_g[:, None] * rows_dy.astype(jnp.float32)).astype(jnp.bfloat16)
        grad_hidden = jnp.dot(scaled, wd.T, preferred_element_type=jnp.float32)
        grad_gate_pre = (grad_hidden * pre_up * sigma * (1.0 + pre_gate * (1.0 - sigma))).astype(jnp.bfloat16)
        grad_up_pre = (grad_hidden * pre_gate * sigma).astype(jnp.bfloat16)
        row_grad = (jnp.dot(grad_gate_pre, wg, preferred_element_type=jnp.float32)
                    + jnp.dot(grad_up_pre, wu, preferred_element_type=jnp.float32)).astype(jnp.bfloat16)
        grad_acc = grad_acc.at[owner].add(jnp.where(valid[:, None], row_grad.astype(jnp.float32), jnp.float32(0.0)))
        gate_acc = gate_acc.at[safe].add(jnp.where(valid, gate_term, jnp.float32(0.0)))
        return (grad_acc, gate_acc), None

    start = (jnp.zeros((TOKENS, D), jnp.float32), jnp.zeros((TOKENS * TOP_K,), jnp.float32))
    (grad_acc, gate_acc), unused = lax.scan(step, start, (table, w_gate, w_up, w_down))
    return grad_acc.astype(jnp.bfloat16), gate_acc.reshape(TOKENS, TOP_K)
```

```python
import functools

import jax
import jax.numpy as jnp
from jax import lax
from jax.experimental import pallas as pl
from jax.experimental.pallas import tpu as pltpu
from jax.sharding import Mesh, PartitionSpec as P

AXES = ("zl", "x", "y", "zh", "c")
PLANE = ("y", "x", "c")
RING = ("zh", "zl")
SIZES = (4, 4, 4, 4, 2)
F32 = jnp.float32
BF16 = jnp.bfloat16

SHIFT = ((-6, 0, 0, 6), (-4, -2, 2, 4), (-2, -4, 4, 2), (0, -6, 6, 0))


def flat_index(zl, x, y, zh, c):
    return (((zl * 4 + x) * 4 + y) * 4 + zh) * 2 + c


def spread_pairs():
    pairs = []
    for zl in range(4):
        for x in range(4):
            for y in range(4):
                for zh in range(4):
                    for c in range(2):
                        z = (zh * 4 + zl + SHIFT[x][zl]) % 16
                        pairs.append(
                            (flat_index(zl, x, y, zh, c), flat_index(z % 4, zh, y, z // 4, c))
                        )
    return pairs


def dot_t(a, b):
    return lax.dot_general(a, b, (((1,), (1,)), ((), ())), preferred_element_type=F32)


def expert_kernel(steps, width, rows_ref, w_ref, out_ref, acc, gate):
    step = pl.program_id(0)
    slabs, height, _ = w_ref.shape
    third = height // 3
    hid = slabs * third
    x = rows_ref[:, :width]
    dy = rows_ref[:, width:]
    wg = w_ref[:, 0:third, :].reshape(hid, width)
    wu = w_ref[:, third : 2 * third, :].reshape(hid, width)
    wd = w_ref[:, 2 * third : 3 * third, :].reshape(hid, width)
    pre_gate = dot_t(x, wg)
    pre_up = dot_t(x, wu)
    q = dot_t(dy, wd)
    sigma = jax.nn.sigmoid(pre_gate)
    act = pre_gate * sigma
    hidden = (act * pre_up).astype(BF16).astype(F32)
    grad_gate = (q * pre_up * sigma * (1.0 + pre_gate * (1.0 - sigma))).astype(BF16)
    grad_up = (q * act).astype(BF16)
    back = jnp.dot(grad_gate, wg, preferred_element_type=F32)
    back = back + jnp.dot(grad_up, wu, preferred_element_type=F32)
    term = jnp.sum(hidden * q, axis=1, keepdims=True)

    @pl.when(step == 0)
    def _():
        acc[...] = back
        gate[...] = term

    @pl.when(step > 0)
    def _():
        acc[...] += back
        gate[...] += term

    @pl.when(step == steps - 1)
    def _():
        out_ref[:, :width] = acc[...].astype(BF16)
        whole = gate[...]
        high = whole.astype(BF16).astype(F32)
        lane = lax.broadcasted_iota(jnp.int32, (whole.shape[0], 128), 1)
        tail = jnp.where(lane == 0, high, jnp.where(lane == 1, whole - high, 0.0))
        out_ref[:, width:] = tail.astype(BF16)


def expert_layer(rows, slabs):
    count, wide = rows.shape
    width = wide // 2
    planes, height, _ = slabs.shape
    steps = 4
    return pl.pallas_call(
        functools.partial(expert_kernel, steps, width),
        grid=(steps,),
        out_shape=jax.ShapeDtypeStruct((count, width + 128), BF16),
        in_specs=[
            pl.BlockSpec((count, wide), lambda i: (0, 0)),
            pl.BlockSpec((planes // steps, height, width), lambda i: (i, 0, 0)),
        ],
        out_specs=pl.BlockSpec((count, width + 128), lambda i: (0, 0)),
        scratch_shapes=[pltpu.VMEM((count, width), F32), pltpu.VMEM((count, 1), F32)],
        compiler_params=pltpu.CompilerParams(vmem_limit_bytes=48 * 1024 * 1024),
    )(rows, slabs)


def local(tokens, cotangent, expert_ids, gate_values, w_gate, w_up, w_down):
    tok_rows, width = tokens.shape
    experts, slots = 32, 9
    places = experts * slots

    slab = jnp.concatenate([w_gate[0], w_up[0], w_down[0]], axis=0)
    slab = lax.ppermute(slab, AXES, spread_pairs())
    slabs = lax.all_gather(slab, RING, axis=0, tiled=False)

    names = jnp.arange(experts, dtype=jnp.int32)
    pick = (expert_ids[:, :, None] == names[None, None, :]).astype(F32)
    member = jnp.sum(pick, axis=1)
    row = jnp.arange(tok_rows, dtype=jnp.int32)
    earlier = (row[None, :] < row[:, None]).astype(BF16)
    before = jnp.dot(earlier, member.astype(BF16), preferred_element_type=F32)
    slot = jnp.sum(before[:, None, :] * pick, axis=2).astype(jnp.int32)
    place = expert_ids * slots + slot
    spots = jnp.arange(places, dtype=jnp.int32)
    send_pick = (
        (place[:, 0][None, :] == spots[:, None]) | (place[:, 1][None, :] == spots[:, None])
    ).astype(BF16)
    both = jnp.concatenate([tokens, cotangent], axis=1)
    send = jnp.dot(send_pick, both, preferred_element_type=F32).astype(BF16)
    rows = lax.all_to_all(
        send.reshape(experts, slots, 2 * width), PLANE, split_axis=0, concat_axis=0, tiled=True
    )

    back = expert_layer(rows.reshape(places, 2 * width), slabs)
    home = lax.all_to_all(
        back.reshape(experts, slots, width + 128), PLANE, split_axis=0, concat_axis=0, tiled=True
    ).reshape(places, width + 128)

    first = (place[:, 0][:, None] == spots[None, :]).astype(F32)
    second = (place[:, 1][:, None] == spots[None, :]).astype(F32)
    weight = first * gate_values[:, 0:1] + second * gate_values[:, 1:2]
    high = weight.astype(BF16)
    low = (weight - high.astype(F32)).astype(BF16)
    grads = home[:, :width]
    token_grad = jnp.dot(high, grads, preferred_element_type=F32)
    token_grad = token_grad + jnp.dot(low, grads, preferred_element_type=F32)
    terms = home[:, width:]
    gates = [
        jnp.sum(jnp.dot(hot.astype(BF16), terms, preferred_element_type=F32), axis=1)
        for hot in (first, second)
    ]
    return token_grad.astype(BF16), jnp.stack(gates, axis=1)


def solution(mesh):
    fine = Mesh(mesh.devices.reshape(SIZES), AXES)
    rows = P(AXES, None)
    weights = P(("y", "zh", "c"), ("zl", "x"), None)
    return jax.shard_map(
        local,
        mesh=fine,
        in_specs=(rows, rows, rows, rows, weights, weights, weights),
        out_specs=(rows, rows),
        check_vma=False,
    )
```

```python
import jax
import jax.numpy as jnp
from jax import lax
from jax.experimental import pallas as pl
from jax.experimental.pallas import tpu as pltpu
from jax.sharding import Mesh, PartitionSpec as P

AXES = ("zl", "x", "y", "zh", "c")
PLANE = ("y", "x", "c")
RING = ("zh", "zl")
SIZES = (4, 4, 4, 4, 2)
EXPERTS = 32
LANES = 8
MAIN = EXPERTS * LANES
F32 = jnp.float32
BF16 = jnp.bfloat16

SHIFT = ((-6, 0, 0, 6), (-4, -2, 2, 4), (-2, -4, 4, 2), (0, -6, 6, 0))


def flat_index(zl, x, y, zh, c):
    return (((zl * 4 + x) * 4 + y) * 4 + zh) * 2 + c


def spread_pairs():
    pairs = []
    for zl in range(4):
        for x in range(4):
            for y in range(4):
                for zh in range(4):
                    for c in range(2):
                        z = (zh * 4 + zl + SHIFT[x][zl]) % 16
                        pairs.append(
                            (flat_index(zl, x, y, zh, c), flat_index(z % 4, zh, y, z // 4, c))
                        )
    return pairs


def dot(a, b):
    return jnp.dot(a, b, preferred_element_type=F32)


def dot_t(a, b):
    return lax.dot_general(a, b, (((1,), (1,)), ((), ())), preferred_element_type=F32)


def iota(shape, axis):
    return lax.broadcasted_iota(jnp.int32, shape, axis)


def split(value):
    high = value.astype(BF16).astype(F32)
    return high, value - high


def piece(i):
    return (384 * i, 384) if i < 4 else (1536 + 256 * (i - 4), 256)


def expert_kernel(rows_ref, slabs_ref, out_ref, weights, grads, sems):
    planes, height, width = slabs_ref.shape
    third = height // 3
    hid = planes * third

    def copy(plane, kind):
        return pltpu.make_async_copy(
            slabs_ref.at[plane, kind * third : (kind + 1) * third, :],
            weights.at[kind, plane * third : (plane + 1) * third, :],
            sems.at[kind, plane],
        )

    def arrive(kind):
        for plane in range(planes):
            copy(plane, kind).wait()

    for kind in (2, 0, 1):
        for plane in range(planes):
            copy(plane, kind).start()

    x = rows_ref[:, :width]
    arrive(2)
    q = dot_t(rows_ref[:, width:], weights[2])
    arrive(0)
    pre_gate = dot_t(x, weights[0])
    arrive(1)
    pre_up = dot_t(x, weights[1])
    sigma = jax.nn.sigmoid(pre_gate)
    act = pre_gate * sigma
    hidden = (act * pre_up).astype(BF16).astype(F32)
    grads[:, :hid] = (q * pre_up * sigma * (1.0 + pre_gate * (1.0 - sigma))).astype(BF16)
    grads[:, hid:] = (q * act).astype(BF16)
    term = jnp.sum(hidden * q, axis=1, keepdims=True)

    back = dot(grads[...], weights[0:2].reshape(2 * hid, width)).astype(BF16)
    out_ref[:, :width] = back[:MAIN]
    ninth = back[MAIN:]
    row, expert = iota((MAIN, EXPERTS), 0), iota((MAIN, EXPERTS), 1)
    two = jnp.zeros((MAIN, 256), F32)
    one = jnp.zeros((MAIN, 128), F32)
    for i in range(LANES):
        at, count = piece(i)
        got = dot((row == expert * LANES + i).astype(BF16), ninth[:, at : at + count])
        two = two + got[:, :256]
        if count == 384:
            one = one + got[:, 256:]
    high, low = split(term)
    lane, slot = iota((MAIN, 128), 1), iota((MAIN, 128), 0) % LANES
    kept = jnp.where(
        lane == slot, high[:MAIN], jnp.where(lane == slot + LANES, low[:MAIN], 0.0)
    ).astype(BF16)
    lane = iota((EXPERTS, 128), 1)
    last = jnp.where(
        lane == 16, high[MAIN:], jnp.where(lane == 17, low[MAIN:], 0.0)
    ).astype(BF16)
    to, come = iota((MAIN, MAIN), 0), iota((MAIN, MAIN), 1)
    gather = ((to % LANES == 4) & (to // LANES == come // LANES)).astype(BF16)
    one = one + dot(gather, kept) + dot((row == expert * LANES + 4).astype(BF16), last)
    out_ref[:, width : width + 256] = two.astype(BF16)
    out_ref[:, width + 256 :] = one.astype(BF16)


def expert_layer(rows, slabs):
    count, wide = rows.shape
    width = wide // 2
    planes, height, _ = slabs.shape
    hid = planes * height // 3
    return pl.pallas_call(
        expert_kernel,
        out_shape=jax.ShapeDtypeStruct((MAIN, width + 384), BF16),
        in_specs=[
            pl.BlockSpec(memory_space=pltpu.VMEM),
            pl.BlockSpec(memory_space=pl.ANY),
        ],
        out_specs=pl.BlockSpec(memory_space=pltpu.VMEM),
        scratch_shapes=[
            pltpu.VMEM((3, hid, width), BF16),
            pltpu.VMEM((count, 2 * hid), BF16),
            pltpu.SemaphoreType.DMA((3, planes)),
        ],
        compiler_params=pltpu.CompilerParams(vmem_limit_bytes=56 * 1024 * 1024),
    )(rows, slabs)


def home_kernel(home_ref, base_ref, slot_ref, gates_ref, grad_ref, term_ref):
    tok_rows, width = grad_ref.shape
    base, slot, gates = base_ref[...], slot_ref[...], gates_ref[...]
    col = iota((tok_rows, MAIN), 1)

    def weights(at):
        total = jnp.zeros((tok_rows, MAIN), F32)
        for k in range(2):
            total = total + jnp.where(col == at[:, k : k + 1], gates[:, k : k + 1], 0.0)
        return jnp.concatenate([part.astype(BF16) for part in split(total)], axis=0)

    def both(got):
        return got[:tok_rows] + got[tok_rows:]

    main = weights(jnp.where(slot < LANES, base + slot, -1))
    ninth_at = jnp.where(slot < LANES, -1000, base)
    for i in range(LANES):
        at, count = piece(i)
        got = dot(main, home_ref[:, at : at + count])
        got = got + dot(weights(ninth_at + i), home_ref[:, width : width + count])
        grad_ref[:, at : at + count] = both(got).astype(BF16)
    lane = iota((tok_rows, 128), 1)
    terms = []
    for k in range(2):
        got = dot((col == base[:, k : k + 1] + 4).astype(BF16), home_ref[:, width + 256 :])
        mine = slot[:, k : k + 1]
        low = jnp.where(mine < LANES, mine + LANES, 17)
        high = jnp.where(mine < LANES, mine, 16)
        terms.append(jnp.sum(jnp.where((lane == high) | (lane == low), got, 0.0), axis=1, keepdims=True))
    term_ref[...] = jnp.where(iota((tok_rows, 2), 1) == 0, terms[0], terms[1])


def bring_home(home, base, slot, gates, width):
    tok_rows = base.shape[0]
    return pl.pallas_call(
        home_kernel,
        out_shape=(
            jax.ShapeDtypeStruct((tok_rows, width), BF16),
            jax.ShapeDtypeStruct((tok_rows, 2), F32),
        ),
        in_specs=[pl.BlockSpec(memory_space=pltpu.VMEM)] * 4,
        out_specs=[pl.BlockSpec(memory_space=pltpu.VMEM)] * 2,
        compiler_params=pltpu.CompilerParams(vmem_limit_bytes=32 * 1024 * 1024),
    )(home, base, slot, gates)


def exchange(wire):
    sent = wire.reshape(EXPERTS, LANES, wire.shape[1])
    got = lax.all_to_all(sent, PLANE, split_axis=0, concat_axis=0, tiled=True)
    return got.reshape(wire.shape)


def local(tokens, cotangent, expert_ids, gate_values, w_gate, w_up, w_down):
    tok_rows, width = tokens.shape

    slab = jnp.concatenate([w_gate[0], w_up[0], w_down[0]], axis=0)
    slab = lax.ppermute(slab, AXES, spread_pairs())
    slabs = lax.all_gather(slab, RING, axis=0, tiled=False)

    names = jnp.arange(EXPERTS, dtype=jnp.int32)
    pick = (expert_ids[:, :, None] == names[None, None, :]).astype(F32)
    member = jnp.sum(pick, axis=1)
    row = jnp.arange(tok_rows, dtype=jnp.int32)
    earlier = (row[None, :] < row[:, None]).astype(BF16)
    before = dot(earlier, member.astype(BF16))
    slot = jnp.sum(before[:, None, :] * pick, axis=2).astype(jnp.int32)
    base = expert_ids * LANES

    spots = jnp.arange(MAIN, dtype=jnp.int32)[:, None]
    main_at = jnp.where(slot < LANES, base + slot, -1)
    ninth_at = jnp.where(slot < LANES, -1, expert_ids)
    main_pick = ((spots == main_at[None, :, 0]) | (spots == main_at[None, :, 1])).astype(BF16)
    heads = names[:, None]
    ninth_pick = ((heads == ninth_at[None, :, 0]) | (heads == ninth_at[None, :, 1])).astype(BF16)
    both = jnp.concatenate([tokens, cotangent], axis=1)
    main = dot(main_pick, both).astype(BF16)
    ninth = dot(ninth_pick, both).astype(BF16).reshape(MAIN, 2 * width // LANES)
    wire = exchange(jnp.concatenate([main, ninth], axis=1))
    rows = jnp.concatenate(
        [wire[:, : 2 * width], wire[:, 2 * width :].reshape(EXPERTS, 2 * width)], axis=0
    )

    home = exchange(expert_layer(rows, slabs))
    return bring_home(home, base, slot, gate_values, width)


def solution(mesh):
    fine = Mesh(mesh.devices.reshape(SIZES), AXES)
    rows = P(AXES, None)
    weights = P(("y", "zh", "c"), ("zl", "x"), None)
    return jax.shard_map(
        local,
        mesh=fine,
        in_specs=(rows, rows, rows, rows, weights, weights, weights),
        out_specs=(rows, rows),
        check_vma=False,
    )
```

```python
import functools

import jax
import jax.numpy as jnp
from jax import lax
from jax.experimental import pallas as pl
from jax.experimental.pallas import tpu as pltpu
from jax.sharding import Mesh, PartitionSpec as P

AXES = ("zl", "x", "y", "zh", "c")
PLANE = ("y", "x", "c")
RING = ("zh", "zl")
SIZES = (4, 4, 4, 4, 2)
EXPERTS = 32
LANES = 8
MAIN = EXPERTS * LANES
VMEM_BYTES = 56 * 1024 * 1024
PARTS = ((0, 16),)
F32 = jnp.float32
BF16 = jnp.bfloat16

SHIFT = ((-6, 0, 0, 6), (-4, -2, 2, 4), (-2, -4, 4, 2), (0, -6, 6, 0))


def flat_index(zl, x, y, zh, c):
    return (((zl * 4 + x) * 4 + y) * 4 + zh) * 2 + c


def spread_pairs():
    pairs = []
    for zl in range(4):
        for x in range(4):
            for y in range(4):
                for zh in range(4):
                    for c in range(2):
                        z = (zh * 4 + zl + SHIFT[x][zl]) % 16
                        pairs.append(
                            (flat_index(zl, x, y, zh, c), flat_index(z % 4, zh, y, z // 4, c))
                        )
    return pairs


def ring_pairs(step):
    pairs = []
    for zl in range(4):
        for x in range(4):
            for y in range(4):
                for zh in range(4):
                    for c in range(2):
                        z = (zh * 4 + zl + step) % 16
                        pairs.append(
                            (flat_index(zl, x, y, zh, c), flat_index(z % 4, x, y, z // 4, c))
                        )
    return pairs


def dot(a, b):
    return jnp.dot(a, b, preferred_element_type=F32)


def dot_t(a, b):
    return lax.dot_general(a, b, (((1,), (1,)), ((), ())), preferred_element_type=F32)


def iota(shape, axis):
    return lax.broadcasted_iota(jnp.int32, shape, axis)


def split(value):
    high = value.astype(BF16).astype(F32)
    return high, value - high


def piece(i):
    return (384 * i, 384) if i < 4 else (1536 + 256 * (i - 4), 256)


def back_wire(back, term, out_ref):
    width = back.shape[1]
    ninth = back[MAIN:]
    out_ref[:, :width] = back[:MAIN]
    row, expert = iota((MAIN, EXPERTS), 0), iota((MAIN, EXPERTS), 1)
    two = jnp.zeros((MAIN, 256), F32)
    one = jnp.zeros((MAIN, 128), F32)
    for i in range(LANES):
        at, count = piece(i)
        got = dot((row == expert * LANES + i).astype(BF16), ninth[:, at : at + count])
        two = two + got[:, :256]
        if count == 384:
            one = one + got[:, 256:]
    high, low = split(term)
    lane, slot = iota((MAIN, 128), 1), iota((MAIN, 128), 0) % LANES
    kept = jnp.where(
        lane == slot, high[:MAIN], jnp.where(lane == slot + LANES, low[:MAIN], 0.0)
    ).astype(BF16)
    lane = iota((EXPERTS, 128), 1)
    last = jnp.where(
        lane == 16, high[MAIN:], jnp.where(lane == 17, low[MAIN:], 0.0)
    ).astype(BF16)
    to, come = iota((MAIN, MAIN), 0), iota((MAIN, MAIN), 1)
    gather = ((to % LANES == 4) & (to // LANES == come // LANES)).astype(BF16)
    one = one + dot(gather, kept) + dot((row == expert * LANES + 4).astype(BF16), last)
    out_ref[:, width : width + 256] = two.astype(BF16)
    out_ref[:, width + 256 :] = one.astype(BF16)


def take_rows(x_wire, dy_wire, x, dy):
    width = x.shape[1]
    part = width // 4
    x[:MAIN, :] = x_wire[:, :width]
    dy[:MAIN, :] = dy_wire[:, :width]
    sender, row = iota((EXPERTS, MAIN), 0), iota((EXPERTS, MAIN), 1)
    for i in range(LANES):
        hot = (row == sender * LANES + i).astype(BF16)
        ref, at = (x, i * part) if i < 4 else (dy, (i - 4) * part)
        ref[MAIN:, at : at + 384] = dot(hot, x_wire[:, width:]).astype(BF16)
        ref[MAIN:, at + 384 : at + part] = dot(hot, dy_wire[:, width:]).astype(BF16)


def expert_kernel(count, first, last, *refs):
    refs = list(refs)
    x_wire, dy_wire = refs.pop(0), refs.pop(0)
    slices = [(refs.pop(0), refs.pop(0)) for _ in range(count)]
    if not first:
        total_in, term_in = refs.pop(0), refs.pop(0)
    if last:
        out_ref = refs.pop(0)
    else:
        total_out, term_out = refs.pop(0), refs.pop(0)
    weights, grads, x, dy, sems = refs[:5]
    height, half = slices[0][0].shape
    third = height // 3
    hid, width = count * third, 2 * half

    def copies(kind):
        return [
            pltpu.make_async_copy(
                slices[n][h].at[kind * third : (kind + 1) * third, :],
                weights.at[kind, n * third : (n + 1) * third, h * half : (h + 1) * half],
                sems.at[kind, n, h],
            )
            for n in range(count)
            for h in range(2)
        ]

    def arrive(kind):
        for copy in copies(kind):
            copy.wait()

    for kind in (2, 0, 1):
        for copy in copies(kind):
            copy.start()
    if not first:
        held, held_sem = refs[5:]
        fetch = pltpu.make_async_copy(total_in, held, held_sem)
        fetch.start()

    take_rows(x_wire, dy_wire, x, dy)
    arrive(2)
    q = dot_t(dy[...], weights[2])
    arrive(0)
    pre_gate = dot_t(x[...], weights[0])
    arrive(1)
    pre_up = dot_t(x[...], weights[1])
    sigma = jax.nn.sigmoid(pre_gate)
    act = pre_gate * sigma
    hidden = (act * pre_up).astype(BF16).astype(F32)
    grads[:, :hid] = (q * pre_up * sigma * (1.0 + pre_gate * (1.0 - sigma))).astype(BF16)
    grads[:, hid:] = (q * act).astype(BF16)
    term = jnp.sum(hidden * q, axis=1, keepdims=True)
    back = dot(grads[...], weights[0:2].reshape(2 * hid, width))
    if not first:
        fetch.wait()
        back = back + held[...]
        term = term + term_in[...]
    if last:
        back_wire(back.astype(BF16), term, out_ref)
    else:
        total_out[...] = back
        term_out[...] = term


def expert_part(wires, slices, before, last):
    places, width = MAIN + EXPERTS, 2 * slices[0][0].shape[1]
    count = len(slices)
    hid = count * slices[0][0].shape[0] // 3
    first = before is None
    vmem, hbm = pl.BlockSpec(memory_space=pltpu.VMEM), pl.BlockSpec(memory_space=pl.ANY)
    if last:
        out_shape = jax.ShapeDtypeStruct((MAIN, width + 384), BF16)
        out_specs = vmem
    else:
        out_shape = (
            jax.ShapeDtypeStruct((places, width), F32),
            jax.ShapeDtypeStruct((places, 1), F32),
        )
        out_specs = (vmem, vmem)
    scratch = [
        pltpu.VMEM((3, hid, width), BF16),
        pltpu.VMEM((places, 2 * hid), BF16),
        pltpu.VMEM((places, width), BF16),
        pltpu.VMEM((places, width), BF16),
        pltpu.SemaphoreType.DMA((3, count, 2)),
    ]
    if not first:
        scratch += [pltpu.VMEM((places, width), F32), pltpu.SemaphoreType.DMA]
    operands = list(wires) + [half for pair in slices for half in pair]
    in_specs = [vmem] * 2 + [hbm] * (2 * count)
    if not first:
        operands += list(before)
        in_specs += [hbm, vmem]
    return pl.pallas_call(
        functools.partial(expert_kernel, count, first, last),
        out_shape=out_shape,
        in_specs=in_specs,
        out_specs=out_specs,
        scratch_shapes=scratch,
        compiler_params=pltpu.CompilerParams(vmem_limit_bytes=VMEM_BYTES),
    )(*operands)


def home_kernel(home_ref, base_ref, slot_ref, gates_ref, grad_ref, term_ref):
    tok_rows, width = grad_ref.shape
    base, slot, gates = base_ref[...], slot_ref[...], gates_ref[...]
    col = iota((tok_rows, MAIN), 1)

    def weights(at):
        total = jnp.zeros((tok_rows, MAIN), F32)
        for k in range(2):
            total = total + jnp.where(col == at[:, k : k + 1], gates[:, k : k + 1], 0.0)
        return jnp.concatenate([part.astype(BF16) for part in split(total)], axis=0)

    def both(got):
        return got[:tok_rows] + got[tok_rows:]

    main = weights(jnp.where(slot < LANES, base + slot, -1))
    ninth_at = jnp.where(slot < LANES, -1000, base)
    for i in range(LANES):
        at, count = piece(i)
        got = dot(main, home_ref[:, at : at + count])
        got = got + dot(weights(ninth_at + i), home_ref[:, width : width + count])
        grad_ref[:, at : at + count] = both(got).astype(BF16)
    lane = iota((tok_rows, 128), 1)
    terms = []
    for k in range(2):
        got = dot((col == base[:, k : k + 1] + 4).astype(BF16), home_ref[:, width + 256 :])
        mine = slot[:, k : k + 1]
        low = jnp.where(mine < LANES, mine + LANES, 17)
        high = jnp.where(mine < LANES, mine, 16)
        terms.append(jnp.sum(jnp.where((lane == high) | (lane == low), got, 0.0), axis=1, keepdims=True))
    term_ref[...] = jnp.where(iota((tok_rows, 2), 1) == 0, terms[0], terms[1])


def bring_home(home, base, slot, gates, width):
    tok_rows = base.shape[0]
    return pl.pallas_call(
        home_kernel,
        out_shape=(
            jax.ShapeDtypeStruct((tok_rows, width), BF16),
            jax.ShapeDtypeStruct((tok_rows, 2), F32),
        ),
        in_specs=[pl.BlockSpec(memory_space=pltpu.VMEM)] * 4,
        out_specs=[pl.BlockSpec(memory_space=pltpu.VMEM)] * 2,
        compiler_params=pltpu.CompilerParams(vmem_limit_bytes=32 * 1024 * 1024),
    )(home, base, slot, gates)


def send_kernel(tokens_ref, cotangent_ref, ids_ref, x_ref, dy_ref, base_ref, slot_ref):
    tok_rows, width = tokens_ref.shape
    ids = ids_ref[...]
    lane = iota((tok_rows, 128), 1)
    picks = [(lane == ids[:, k : k + 1]).astype(F32) for k in range(2)]
    earlier = (iota((tok_rows, tok_rows), 1) < iota((tok_rows, tok_rows), 0)).astype(BF16)
    before = dot(earlier, (picks[0] + picks[1]).astype(BF16))
    slots = [jnp.sum(before * pick, axis=1, keepdims=True).astype(jnp.int32) for pick in picks]
    slot = jnp.where(iota((tok_rows, 2), 1) == 0, slots[0], slots[1])
    base = ids * LANES
    base_ref[...] = base
    slot_ref[...] = slot
    col = iota((tok_rows, MAIN), 1)
    main_at = jnp.where(slot < LANES, base + slot, -1)
    ninth_at = jnp.where(slot < LANES, -1, ids)
    main = ((col == main_at[:, 0:1]) | (col == main_at[:, 1:2])).astype(F32).T.astype(BF16)
    ninth = ((lane == ninth_at[:, 0:1]) | (lane == ninth_at[:, 1:2])).astype(F32).T[:EXPERTS]
    ninth = ninth.astype(BF16)
    row, expert = iota((MAIN, EXPERTS), 0), iota((MAIN, EXPERTS), 1)
    part = width // 4
    beside = jnp.zeros((MAIN, part), F32)
    for which, ref in enumerate((tokens_ref, cotangent_ref)):
        last = dot(ninth, ref[...]).astype(BF16)
        for i in range(4):
            hot = (row == expert * LANES + 4 * which + i).astype(BF16)
            beside = beside + dot(hot, last[:, i * part : (i + 1) * part])
    x_ref[:, :width] = dot(main, tokens_ref[...]).astype(BF16)
    dy_ref[:, :width] = dot(main, cotangent_ref[...]).astype(BF16)
    x_ref[:, width:] = beside[:, :384].astype(BF16)
    dy_ref[:, width:] = beside[:, 384:].astype(BF16)


def send_rows(tokens, cotangent, expert_ids):
    tok_rows, width = tokens.shape
    vmem = pl.BlockSpec(memory_space=pltpu.VMEM)
    return pl.pallas_call(
        send_kernel,
        out_shape=(
            jax.ShapeDtypeStruct((MAIN, width + 384), BF16),
            jax.ShapeDtypeStruct((MAIN, width + 256), BF16),
            jax.ShapeDtypeStruct((tok_rows, 2), jnp.int32),
            jax.ShapeDtypeStruct((tok_rows, 2), jnp.int32),
        ),
        in_specs=[vmem] * 3,
        out_specs=[vmem] * 4,
        compiler_params=pltpu.CompilerParams(vmem_limit_bytes=VMEM_BYTES),
    )(tokens, cotangent, expert_ids)


def exchange(wire):
    sent = wire.reshape(EXPERTS, LANES, wire.shape[1])
    got = lax.all_to_all(sent, PLANE, split_axis=0, concat_axis=0, tiled=True)
    return got.reshape(wire.shape)


def local(tokens, cotangent, expert_ids, gate_values, w_gate, w_up, w_down):
    tok_rows, width = tokens.shape

    slab = jnp.concatenate([w_gate[0], w_up[0], w_down[0]], axis=0)
    spread, up, down = spread_pairs(), ring_pairs(1), ring_pairs(-1)
    half = width // 2
    right = [lax.ppermute(part, AXES, spread) for part in (slab[:, :half], slab[:, half:])]
    x_wire, dy_wire, base, slot = send_rows(tokens, cotangent, expert_ids)
    dy_wire, right[0] = lax.optimization_barrier((dy_wire, right[0]))
    left = right
    slices = [right]
    for _ in range(7):
        right = [lax.ppermute(part, AXES, up) for part in right]
        left = [lax.ppermute(part, AXES, down) for part in left]
        slices += [right, left]
    slices.append([lax.ppermute(right[0], AXES, up), lax.ppermute(left[1], AXES, down)])

    wires = exchange(x_wire), exchange(dy_wire)
    total = None
    for begin, end in PARTS:
        total = expert_part(wires, slices[begin:end], total, end == len(slices))
    return bring_home(exchange(total), base, slot, gate_values, width)


def solution(mesh):
    fine = Mesh(mesh.devices.reshape(SIZES), AXES)
    rows = P(AXES, None)
    weights = P(("y", "zh", "c"), ("zl", "x"), None)
    return jax.shard_map(
        local,
        mesh=fine,
        in_specs=(rows, rows, rows, rows, weights, weights, weights),
        out_specs=(rows, rows),
        check_vma=False,
    )
```

```python
import functools

import jax
import jax.numpy as jnp
from jax import lax
from jax.experimental import pallas as pl
from jax.experimental.pallas import tpu as pltpu
from jax.sharding import Mesh, PartitionSpec as P

AXES = ("zl", "x", "y", "zh", "c")
PLANE = ("y", "x", "c")
RING = ("zh", "zl")
SIZES = (4, 4, 4, 4, 2)
EXPERTS = 32
LANES = 8
MAIN = EXPERTS * LANES
VMEM_BYTES = 56 * 1024 * 1024
PARTS = ((0, 16),)
F32 = jnp.float32
BF16 = jnp.bfloat16

SHIFT = ((-6, 0, 0, 6), (-4, -2, 2, 4), (-2, -4, 4, 2), (0, -6, 6, 0))


def flat_index(zl, x, y, zh, c):
    return (((zl * 4 + x) * 4 + y) * 4 + zh) * 2 + c


def spread_pairs():
    pairs = []
    for zl in range(4):
        for x in range(4):
            for y in range(4):
                for zh in range(4):
                    for c in range(2):
                        z = (zh * 4 + zl + SHIFT[x][zl]) % 16
                        pairs.append(
                            (flat_index(zl, x, y, zh, c), flat_index(z % 4, zh, y, z // 4, c))
                        )
    return pairs


def ring_pairs(step):
    pairs = []
    for zl in range(4):
        for x in range(4):
            for y in range(4):
                for zh in range(4):
                    for c in range(2):
                        z = (zh * 4 + zl + step) % 16
                        pairs.append(
                            (flat_index(zl, x, y, zh, c), flat_index(z % 4, x, y, z // 4, c))
                        )
    return pairs


def dot(a, b):
    return jnp.dot(a, b, preferred_element_type=F32)


def dot_t(a, b):
    return lax.dot_general(a, b, (((1,), (1,)), ((), ())), preferred_element_type=F32)


def iota(shape, axis):
    return lax.broadcasted_iota(jnp.int32, shape, axis)


def split(value):
    high = value.astype(BF16).astype(F32)
    return high, value - high


def piece(i):
    return (384 * i, 384) if i < 4 else (1536 + 256 * (i - 4), 256)


def back_wire(back, term, out_ref):
    width = back.shape[1]
    ninth = back[MAIN:]
    out_ref[:, :width] = back[:MAIN]
    row, expert = iota((MAIN, EXPERTS), 0), iota((MAIN, EXPERTS), 1)
    two = jnp.zeros((MAIN, 256), F32)
    one = jnp.zeros((MAIN, 128), F32)
    for i in range(LANES):
        at, count = piece(i)
        got = dot((row == expert * LANES + i).astype(BF16), ninth[:, at : at + count])
        two = two + got[:, :256]
        if count == 384:
            one = one + got[:, 256:]
    high, low = split(term)
    lane, slot = iota((MAIN, 128), 1), iota((MAIN, 128), 0) % LANES
    kept = jnp.where(
        lane == slot, high[:MAIN], jnp.where(lane == slot + LANES, low[:MAIN], 0.0)
    ).astype(BF16)
    lane = iota((EXPERTS, 128), 1)
    last = jnp.where(
        lane == 16, high[MAIN:], jnp.where(lane == 17, low[MAIN:], 0.0)
    ).astype(BF16)
    to, come = iota((MAIN, MAIN), 0), iota((MAIN, MAIN), 1)
    gather = ((to % LANES == 4) & (to // LANES == come // LANES)).astype(BF16)
    one = one + dot(gather, kept) + dot((row == expert * LANES + 4).astype(BF16), last)
    out_ref[:, width : width + 256] = two.astype(BF16)
    out_ref[:, width + 256 :] = one.astype(BF16)


def take_rows(x_wire, dy_wire, x, dy):
    width = x.shape[1]
    part = width // 4
    x[:MAIN, :] = x_wire[:, :width]
    dy[:MAIN, :] = dy_wire[:, :width]
    sender, row = iota((EXPERTS, MAIN), 0), iota((EXPERTS, MAIN), 1)
    for i in range(LANES):
        hot = (row == sender * LANES + i).astype(BF16)
        ref, at = (x, i * part) if i < 4 else (dy, (i - 4) * part)
        ref[MAIN:, at : at + 384] = dot(hot, x_wire[:, width:]).astype(BF16)
        ref[MAIN:, at + 384 : at + part] = dot(hot, dy_wire[:, width:]).astype(BF16)


def expert_kernel(count, first, last, *refs):
    refs = list(refs)
    x_wire, dy_wire = refs.pop(0), refs.pop(0)
    slices = [(refs.pop(0), refs.pop(0)) for _ in range(count)]
    if not first:
        total_in, term_in = refs.pop(0), refs.pop(0)
    if last:
        out_ref = refs.pop(0)
    else:
        total_out, term_out = refs.pop(0), refs.pop(0)
    weights, grads, x, dy, sems = refs[:5]
    height, half = slices[0][0].shape
    third = height // 3
    hid, width = count * third, 2 * half

    def copies(kind):
        return [
            pltpu.make_async_copy(
                slices[n][h].at[kind * third : (kind + 1) * third, :],
                weights.at[kind, n * third : (n + 1) * third, h * half : (h + 1) * half],
                sems.at[kind, n, h],
            )
            for n in range(count)
            for h in range(2)
        ]

    def arrive(kind):
        for copy in copies(kind):
            copy.wait()

    for kind in (2, 0, 1):
        for copy in copies(kind):
            copy.start()
    if not first:
        held, held_sem = refs[5:]
        fetch = pltpu.make_async_copy(total_in, held, held_sem)
        fetch.start()

    take_rows(x_wire, dy_wire, x, dy)
    arrive(2)
    q = dot_t(dy[...], weights[2])
    arrive(0)
    pre_gate = dot_t(x[...], weights[0])
    arrive(1)
    pre_up = dot_t(x[...], weights[1])
    sigma = jax.nn.sigmoid(pre_gate)
    act = pre_gate * sigma
    hidden = (act * pre_up).astype(BF16).astype(F32)
    grads[:, :hid] = (q * pre_up * sigma * (1.0 + pre_gate * (1.0 - sigma))).astype(BF16)
    grads[:, hid:] = (q * act).astype(BF16)
    term = jnp.sum(hidden * q, axis=1, keepdims=True)
    back = dot(grads[...], weights[0:2].reshape(2 * hid, width))
    if not first:
        fetch.wait()
        back = back + held[...]
        term = term + term_in[...]
    if last:
        back_wire(back.astype(BF16), term, out_ref)
    else:
        total_out[...] = back
        term_out[...] = term


def expert_part(wires, slices, before, last):
    places, width = MAIN + EXPERTS, 2 * slices[0][0].shape[1]
    count = len(slices)
    hid = count * slices[0][0].shape[0] // 3
    first = before is None
    vmem, hbm = pl.BlockSpec(memory_space=pltpu.VMEM), pl.BlockSpec(memory_space=pl.ANY)
    if last:
        out_shape = jax.ShapeDtypeStruct((MAIN, width + 384), BF16)
        out_specs = vmem
    else:
        out_shape = (
            jax.ShapeDtypeStruct((places, width), F32),
            jax.ShapeDtypeStruct((places, 1), F32),
        )
        out_specs = (vmem, vmem)
    scratch = [
        pltpu.VMEM((3, hid, width), BF16),
        pltpu.VMEM((places, 2 * hid), BF16),
        pltpu.VMEM((places, width), BF16),
        pltpu.VMEM((places, width), BF16),
        pltpu.SemaphoreType.DMA((3, count, 2)),
    ]
    if not first:
        scratch += [pltpu.VMEM((places, width), F32), pltpu.SemaphoreType.DMA]
    operands = list(wires) + [half for pair in slices for half in pair]
    in_specs = [vmem] * 2 + [hbm] * (2 * count)
    if not first:
        operands += list(before)
        in_specs += [hbm, vmem]
    return pl.pallas_call(
        functools.partial(expert_kernel, count, first, last),
        out_shape=out_shape,
        in_specs=in_specs,
        out_specs=out_specs,
        scratch_shapes=scratch,
        compiler_params=pltpu.CompilerParams(vmem_limit_bytes=VMEM_BYTES),
    )(*operands)


def home_kernel(home_ref, base_ref, slot_ref, gates_ref, grad_ref, term_ref):
    tok_rows, width = grad_ref.shape
    base, slot, gates = base_ref[...], slot_ref[...], gates_ref[...]
    col = iota((tok_rows, MAIN), 1)

    def weights(at):
        total = jnp.zeros((tok_rows, MAIN), F32)
        for k in range(2):
            total = total + jnp.where(col == at[:, k : k + 1], gates[:, k : k + 1], 0.0)
        return jnp.concatenate([part.astype(BF16) for part in split(total)], axis=0)

    def both(got):
        return got[:tok_rows] + got[tok_rows:]

    main = weights(jnp.where(slot < LANES, base + slot, -1))
    ninth_at = jnp.where(slot < LANES, -1000, base)
    for i in range(LANES):
        at, count = piece(i)
        got = dot(main, home_ref[:, at : at + count])
        got = got + dot(weights(ninth_at + i), home_ref[:, width : width + count])
        grad_ref[:, at : at + count] = both(got).astype(BF16)
    lane = iota((tok_rows, 128), 1)
    terms = []
    for k in range(2):
        got = dot((col == base[:, k : k + 1] + 4).astype(BF16), home_ref[:, width + 256 :])
        mine = slot[:, k : k + 1]
        low = jnp.where(mine < LANES, mine + LANES, 17)
        high = jnp.where(mine < LANES, mine, 16)
        terms.append(jnp.sum(jnp.where((lane == high) | (lane == low), got, 0.0), axis=1, keepdims=True))
    term_ref[...] = jnp.where(lane == 0, terms[0], terms[1]).T[:2]


def bring_home(home, base, slot, gates, width):
    tok_rows = base.shape[0]
    return pl.pallas_call(
        home_kernel,
        out_shape=(
            jax.ShapeDtypeStruct((tok_rows, width), BF16),
            jax.ShapeDtypeStruct((2, tok_rows), F32),
        ),
        in_specs=[pl.BlockSpec(memory_space=pltpu.VMEM)] * 4,
        out_specs=[pl.BlockSpec(memory_space=pltpu.VMEM)] * 2,
        compiler_params=pltpu.CompilerParams(vmem_limit_bytes=32 * 1024 * 1024),
    )(home, base, slot, gates)


def send_kernel(tokens_ref, cotangent_ref, ids_ref, x_ref, dy_ref, base_ref, slot_ref):
    tok_rows, width = tokens_ref.shape
    ids = ids_ref[...]
    lane = iota((tok_rows, 128), 1)
    picks = [(lane == ids[:, k : k + 1]).astype(F32) for k in range(2)]
    earlier = (iota((tok_rows, tok_rows), 1) < iota((tok_rows, tok_rows), 0)).astype(BF16)
    before = dot(earlier, (picks[0] + picks[1]).astype(BF16))
    slots = [jnp.sum(before * pick, axis=1, keepdims=True).astype(jnp.int32) for pick in picks]
    slot = jnp.where(iota((tok_rows, 2), 1) == 0, slots[0], slots[1])
    base = ids * LANES
    base_ref[...] = base
    slot_ref[...] = slot
    col = iota((tok_rows, MAIN), 1)
    main_at = jnp.where(slot < LANES, base + slot, -1)
    ninth_at = jnp.where(slot < LANES, -1, ids)
    main = ((col == main_at[:, 0:1]) | (col == main_at[:, 1:2])).astype(F32).T.astype(BF16)
    ninth = ((lane == ninth_at[:, 0:1]) | (lane == ninth_at[:, 1:2])).astype(F32).T[:EXPERTS]
    ninth = ninth.astype(BF16)
    row, expert = iota((MAIN, EXPERTS), 0), iota((MAIN, EXPERTS), 1)
    part = width // 4
    beside = jnp.zeros((MAIN, part), F32)
    for which, ref in enumerate((tokens_ref, cotangent_ref)):
        last = dot(ninth, ref[...]).astype(BF16)
        for i in range(4):
            hot = (row == expert * LANES + 4 * which + i).astype(BF16)
            beside = beside + dot(hot, last[:, i * part : (i + 1) * part])
    x_ref[:, :width] = dot(main, tokens_ref[...]).astype(BF16)
    dy_ref[:, :width] = dot(main, cotangent_ref[...]).astype(BF16)
    x_ref[:, width:] = beside[:, :384].astype(BF16)
    dy_ref[:, width:] = beside[:, 384:].astype(BF16)


def send_rows(tokens, cotangent, expert_ids):
    tok_rows, width = tokens.shape
    vmem = pl.BlockSpec(memory_space=pltpu.VMEM)
    return pl.pallas_call(
        send_kernel,
        out_shape=(
            jax.ShapeDtypeStruct((MAIN, width + 384), BF16),
            jax.ShapeDtypeStruct((MAIN, width + 256), BF16),
            jax.ShapeDtypeStruct((tok_rows, 2), jnp.int32),
            jax.ShapeDtypeStruct((tok_rows, 2), jnp.int32),
        ),
        in_specs=[vmem] * 3,
        out_specs=[vmem] * 4,
        compiler_params=pltpu.CompilerParams(vmem_limit_bytes=VMEM_BYTES),
    )(tokens, cotangent, expert_ids)


def exchange(wire):
    sent = wire.reshape(EXPERTS, LANES, wire.shape[1])
    got = lax.all_to_all(sent, PLANE, split_axis=0, concat_axis=0, tiled=True)
    return got.reshape(wire.shape)


def local(tokens, cotangent, expert_ids, gate_values, w_gate, w_up, w_down):
    tok_rows, width = tokens.shape

    slab = jnp.concatenate([w_gate[0], w_up[0], w_down[0]], axis=0)
    spread, up, down = spread_pairs(), ring_pairs(1), ring_pairs(-1)
    half = width // 2
    right = [lax.ppermute(part, AXES, spread) for part in (slab[:, :half], slab[:, half:])]
    x_wire, dy_wire, base, slot = send_rows(tokens, cotangent, expert_ids)
    dy_wire, right[0] = lax.optimization_barrier((dy_wire, right[0]))
    left = right
    slices = [right]
    for _ in range(7):
        right = [lax.ppermute(part, AXES, up) for part in right]
        left = [lax.ppermute(part, AXES, down) for part in left]
        slices += [right, left]
    slices.append([lax.ppermute(right[0], AXES, up), lax.ppermute(left[1], AXES, down)])

    wires = exchange(x_wire), exchange(dy_wire)
    total = None
    for begin, end in PARTS:
        total = expert_part(wires, slices[begin:end], total, end == len(slices))
    token_grad, terms = bring_home(exchange(total), base, slot, gate_values, width)
    return token_grad, terms.T


def solution(mesh):
    fine = Mesh(mesh.devices.reshape(SIZES), AXES)
    rows = P(AXES, None)
    weights = P(("y", "zh", "c"), ("zl", "x"), None)
    return jax.shard_map(
        local,
        mesh=fine,
        in_specs=(rows, rows, rows, rows, weights, weights, weights),
        out_specs=(rows, rows),
        check_vma=False,
    )
```
